32 devices in a mesh: section: 4 (over x, core), seq: 8 (over z, y).
Axes of the slice: x: 2, y: 2, z: 4, core: 2. Of those that a mesh axis runs over, the one named last changes fastest.
Arguments:
- queries: bfloat16 [2048, 512], P('seq', 'section'), may hold values from -64 to 64
- key_rows: bfloat16 [2048, 512], P('seq', 'section'), may hold values from -64 to 64
- values: bfloat16 [2048, 512], P('seq', 'section'), may hold values from -6 to 6
- out_grad: bfloat16 [2048, 512], P('seq', 'section'), may hold values from -6 to 6
- query_gain: float32 [512], P('section'), may hold values from 1 to 3
- key_gain: float32 [512], P('section'), may hold values from 1 to 3
- stretch_id: int32 [2048], P('seq'), may hold values from 0 to 7, as said below
Outputs:
- attended: bfloat16 [2048, 512], P('seq', 'section')
- grad_queries: float32 [2048, 512], P('seq', 'section')
- grad_keys: float32 [2048, 512], P('seq', 'section')
- grad_values: float32 [2048, 512], P('seq', 'section')
The draws below stay inside these ranges and needn't reach their ends.
Inputs may be any that keep to these rules, and one draw needn't show every extreme that they name: stretch_id never falls along the tokens and changes only at multiples of 128 tokens (whole latent frames); the first frame is stretch 0 alone, stretch 1 spans exactly three frames (384 tokens); from frame 4 on, stretches come in consecutive pairs that together span exactly four frames, each stretch one to three frames.
All inputs are finite; a program needn't handle non-finite values.
Results may differ from the reference program's by a relative error of at most 0.038.
Values may be sent and summed in bfloat16 or wider, within the bound.
A program may use at most 64 MiB of HBM per device.

```python
import math
import jax
import jax.numpy as jnp
from jax import lax

HEAD_DIM = 128
TOK_DEV = 256
HEADS = 4
WIDTH = 512
TOKENS = 2048
FRAME_TOK = 128
N_SEQ = 8


def pair_draw(key):
    width = HEADS * HEAD_DIM
    streams = jax.random.split(key, 5)
    head_of = (jnp.arange(width) // HEAD_DIM).astype(jnp.float32)
    column_scale = jnp.exp(jax.random.uniform(streams[0], (width,), jnp.float32, math.log(0.3), math.log(3.0)))
    query_scale = jnp.exp(jax.random.uniform(streams[1], (TOKENS, 1), jnp.float32, math.log(0.3), math.log(3.0)))
    key_scale = jnp.exp(jax.random.uniform(streams[2], (TOKENS, 1), jnp.float32, math.log(0.3), math.log(3.0)))
    spread = max(HEADS - 1, 1)
    ramp = math.sqrt(3.0) ** (head_of / spread)
    query_base = jnp.clip(jax.random.normal(streams[3], (TOKENS, width), jnp.float32), -4.0, 4.0)
    key_base = jnp.clip(jax.random.normal(streams[4], (TOKENS, width), jnp.float32), -4.0, 4.0)
    query_draw = query_base * column_scale[None, :] * ramp[None, :] * query_scale
    key_draw = key_base * column_scale[None, :] * ramp[None, :] * key_scale
    return (jnp.clip(query_draw, -64.0, 64.0), jnp.clip(key_draw, -64.0, 64.0))


def draw_queries(key, part):
    return pair_draw(jax.random.fold_in(key, 7))[0].astype(jnp.bfloat16)


def draw_key_rows(key, part):
    return pair_draw(jax.random.fold_in(key, 7))[1].astype(jnp.bfloat16)


def draw_stretch_id(key, part):
    frame_count = TOKENS // FRAME_TOK
    group_count = (frame_count - 4) // 4
    picks = jax.random.randint(jax.random.fold_in(key, 11), (group_count,), 0, 3).astype(jnp.int32)
    first_span = (picks + 1).astype(jnp.int32)
    second_span = (4 - first_span).astype(jnp.int32)
    paired = jnp.stack([first_span, second_span], axis=1).reshape(2 * group_count)
    spans = jnp.concatenate([jnp.array([1, 3], jnp.int32), paired.astype(jnp.int32)])
    starts = jnp.cumsum(spans) - spans
    frame_of = (jnp.arange(TOKENS, dtype=jnp.int32) // FRAME_TOK).astype(jnp.int32)
    stretch = jnp.sum((starts[None, :] <= frame_of[:, None]).astype(jnp.int32), axis=1) - 1
    return stretch.astype(jnp.int32)


def level_of(key, shape, shards, smallest, top_value):
    level = 1.0
    for axis_at, shards_of in shards:
        draws = jax.random.uniform(jax.random.fold_in(jax.random.fold_in(key, 6), axis_at), (shards_of,), jnp.float32, smallest / len(shards), top_value / len(shards))
        level = level * jnp.repeat(jnp.exp(draws), shape[axis_at] // shards_of).reshape((-1,) + (1,) * (len(shape) - 1 - axis_at))
    return level


def bell_draw(own_key, dims, scale, limit, shards=(), kind=jnp.bfloat16):
    level = level_of(own_key, dims, shards, -0.22, 0.18) if shards else 1.0
    result = jax.random.normal(own_key, dims, jnp.float32) * scale * level
    return jnp.minimum(jnp.maximum(result, -limit), limit).astype(kind)


def setup_inputs(seed: int = 0) -> dict:
    streams_of = jax.random.split(jax.random.key(seed), 8)
    queries = draw_queries(jax.random.fold_in(streams_of[7], 71), 0)
    key_rows = draw_key_rows(jax.random.fold_in(streams_of[7], 71), 0)
    values = bell_draw(streams_of[2], (TOKENS, WIDTH), 1.0, 6.0, ((0, 8), (1, 4)))
    out_grad = bell_draw(streams_of[3], (TOKENS, WIDTH), 1.0, 6.0, ((0, 8), (1, 4)))
    query_gain = jnp.clip(1.0 + 2.0 * jax.random.uniform(streams_of[4], (WIDTH,), jnp.float32) ** level_of(streams_of[4], (WIDTH,), ((0, 4),), -0.2, 0.2), 1.0, 3.0)
    key_gain = jnp.clip(1.0 + 2.0 * jax.random.uniform(streams_of[5], (WIDTH,), jnp.float32) ** level_of(streams_of[5], (WIDTH,), ((0, 4),), -0.2, 0.2), 1.0, 3.0)
    stretch_id = draw_stretch_id(jax.random.fold_in(streams_of[7], 71), 0)
    return {"queries": queries, "key_rows": key_rows, "values": values, "out_grad": out_grad, "query_gain": query_gain, "key_gain": key_gain, "stretch_id": stretch_id}


EPSILON = 1e-06

def normalize(raw_rows, gain):
    widened = raw_rows.astype(jnp.float32)
    inv_root = lax.rsqrt(lax.optimization_barrier(jnp.mean(widened * widened, axis=1)) + EPSILON)
    normed = (widened * inv_root[:, None] * gain[None, :]).astype(jnp.bfloat16)
    return (widened, inv_root, normed)

def norm_backward(widened, inv_root, gain, grad_hat):
    row_term = lax.optimization_barrier(jnp.sum(grad_hat * gain[None, :] * widened, axis=1))
    return gain[None, :] * inv_root[:, None] * grad_hat - widened * (inv_root ** 3 * row_term / WIDTH)[:, None]

def head_split(matrix):
    return jnp.transpose(matrix.reshape(TOKENS, HEADS, HEAD_DIM), (1, 0, 2))

def head_merge(stacked):
    return jnp.transpose(stacked, (1, 0, 2)).reshape(TOKENS, WIDTH)

def one_head(operands, stretch_id):
    query_hat, key_hat, value_rows, grad_rows = operands
    score_scale = 1.0 / math.sqrt(HEAD_DIM)
    blocked = (query_hat.reshape(N_SEQ, TOK_DEV, HEAD_DIM), grad_rows.reshape(N_SEQ, TOK_DEV, HEAD_DIM), stretch_id.reshape(N_SEQ, TOK_DEV))

    def block_step(carried, block_rows):
        key_grad, value_grad = carried
        query_block, grad_block, stretch_block = block_rows
        scores = jnp.dot(query_block, key_hat.T, preferred_element_type=jnp.float32) * score_scale
        visible = stretch_id[None, :] <= stretch_block[:, None]
        scores = jnp.where(visible, scores, -jnp.inf)
        row_top = lax.optimization_barrier(jnp.max(scores, axis=1))
        weights = jnp.exp(scores - row_top[:, None])
        row_sum = lax.optimization_barrier(jnp.sum(weights, axis=1))
        attended = (jnp.dot(weights.astype(jnp.bfloat16), value_rows, preferred_element_type=jnp.float32) / row_sum[:, None]).astype(jnp.bfloat16)
        log_total = row_top + jnp.log(row_sum)
        row_delta = lax.optimization_barrier(jnp.sum(grad_block.astype(jnp.float32) * attended.astype(jnp.float32), axis=1))
        chances = jnp.exp(scores - log_total[:, None])
        grad_chances = jnp.dot(grad_block, value_rows.T, preferred_element_type=jnp.float32)
        grad_scores = (chances * (grad_chances - row_delta[:, None])).astype(jnp.bfloat16)
        query_grad = jnp.dot(grad_scores, key_hat, preferred_element_type=jnp.float32) * score_scale
        key_grad = key_grad + jnp.dot(grad_scores.T, query_block, preferred_element_type=jnp.float32) * score_scale
        value_grad = value_grad + jnp.dot(chances.astype(jnp.bfloat16).T, grad_block, preferred_element_type=jnp.float32)
        return ((key_grad, value_grad), (attended, query_grad))
    zero_rows = jnp.zeros((TOKENS, HEAD_DIM), jnp.float32)
    (key_grad, value_grad), (attended, query_grad) = lax.scan(block_step, (zero_rows, zero_rows), blocked)
    return (attended.reshape(TOKENS, HEAD_DIM), query_grad.reshape(TOKENS, HEAD_DIM), key_grad, value_grad)

def reference(queries, key_rows, values, out_grad, query_gain, key_gain, stretch_id):
    query_wide, query_root, query_hat = normalize(queries, query_gain)
    key_wide, key_root, key_hat = normalize(key_rows, key_gain)
    operands = (head_split(query_hat), head_split(key_hat), head_split(values), head_split(out_grad))
    attended, query_grad, key_grad, value_grad = lax.map(lambda parts: one_head(parts, stretch_id), operands)
    grad_queries = norm_backward(query_wide, query_root, query_gain, head_merge(query_grad))
    grad_keys = norm_backward(key_wide, key_root, key_gain, head_merge(key_grad))
    return (head_merge(attended), grad_queries, grad_keys, head_merge(value_grad))
```

```python
import functools
import math

import jax
import jax.numpy as jnp
from jax import lax
from jax.experimental import pallas as pl
from jax.experimental.pallas import tpu as pltpu
from jax.sharding import PartitionSpec as P

EPSILON = 1e-06
NEG_FILL = -1e30
FRAME = 128
GROUP_FRAMES = 4
VMEM_BYTES = 60 * 1024 * 1024
V, K, G, Q = range(4)
MESH = pl.DeviceIdType.MESH


def dot(a, b, contract):
    return lax.dot_general(
        a, b, (contract, ((), ())), preferred_element_type=jnp.float32
    )


def nt(a, b):
    return dot(a, b, ((1,), (1,)))


def tn(a, b):
    return dot(a, b, ((0,), (0,)))


def nn(a, b):
    return dot(a, b, ((1,), (0,)))


def kernel(
    n_sec, n,
    q_hbm, k_hbm, v_hbm, g_hbm, q_gain_hbm, k_gain_hbm, stretch_hbm,
    att_hbm, dq_hbm, dk_hbm, dv_hbm,
    q_raw, k_raw, q_gain, k_gain, stretch, vb, kb, gb, qb, partner_stretch, sec, stats, s_buf, dp_buf,
    top, total, acc, dk_acc, dv_acc, att_out, dq_out, dk_out,
    recv, send_z, send_p, stretch_sem, sec_send, sec_recv, stat_send, stat_recv, local,
):
    rows, d = q_raw.shape
    span = 2
    levels = n // span
    width = d * n_sec
    scale = 1.0 / math.sqrt(d)
    log2_scale = scale * math.log2(math.e)
    me = lax.axis_index("seq")
    my_sec = lax.axis_index("section")
    level = me // span
    side = me % span
    partner = me + 1 - 2 * side
    has_up = level < levels - 1
    has_down = level > 0
    bufs = [vb, kb, gb, qb]

    loads = [
        pltpu.make_async_copy(q_hbm, q_raw, local.at[0]),
        pltpu.make_async_copy(k_hbm, k_raw, local.at[1]),
        pltpu.make_async_copy(v_hbm, vb.at[me], local.at[2]),
        pltpu.make_async_copy(g_hbm, gb.at[me], local.at[3]),
        pltpu.make_async_copy(q_gain_hbm, q_gain, local.at[4]),
        pltpu.make_async_copy(k_gain_hbm, k_gain, local.at[5]),
        pltpu.make_async_copy(stretch_hbm, stretch, local.at[6]),
    ]
    for load in loads:
        load.start()

    barrier = pltpu.get_barrier_semaphore()
    for step in range(1, n_sec):
        pl.semaphore_signal(
            barrier, inc=1, device_id={"section": lax.rem(my_sec + step, n_sec)},
            device_id_type=MESH,
        )
    for step in range(1, n):
        pl.semaphore_signal(
            barrier, inc=1, device_id={"seq": lax.rem(me + step, n)}, device_id_type=MESH
        )

    def remote(src, dst, send_sem, recv_sem, device):
        return pltpu.make_async_remote_copy(
            src_ref=src, dst_ref=dst, send_sem=send_sem, recv_sem=recv_sem,
            device_id=device, device_id_type=MESH,
        )

    def z_copy(a, slot, src=None):
        to = me + span if a in (V, K) else me - span
        block = bufs[a].at[slot]
        return remote(
            block if src is None else src, block, send_z.at[a, slot], recv.at[a, slot],
            {"seq": to},
        )

    def p_copy(a, slot, src=None):
        block = bufs[a].at[slot]
        return remote(
            block if src is None else src, block, send_p.at[a, slot], recv.at[a, slot],
            {"seq": partner},
        )

    def onward(a):
        return has_up if a in (V, K) else has_down

    def sec_copy(phase, step):
        return remote(
            sec.at[phase, 0], sec.at[phase, step], sec_send.at[phase, step],
            sec_recv.at[phase, step],
            {"section": lax.rem(my_sec + step, n_sec)},
        )

    def sec_start(phase):
        for step in range(1, n_sec):
            sec_copy(phase, step).start()

    def sec_sum(phase):
        result = sec[phase, 0]
        for step in range(1, n_sec):
            sec_copy(phase, step).wait_recv()
            result = result + sec[phase, step]
        return result

    def row_sum_of(matrix):
        return jnp.sum(matrix.T, axis=0, keepdims=True)

    def as_column(row):
        return jnp.broadcast_to(row, (d, rows)).T

    loads[0].wait()
    loads[1].wait()
    q_wide = q_raw[...].astype(jnp.float32)
    k_wide = k_raw[...].astype(jnp.float32)
    sec[0, 0] = jnp.zeros((8, rows), jnp.float32)
    sec[0, 0, 0:1, :] = row_sum_of(q_wide * q_wide)
    sec[0, 0, 1:2, :] = row_sum_of(k_wide * k_wide)

    pl.semaphore_wait(barrier, n_sec - 1 + n - 1)

    sec_start(0)
    for load in loads[4:]:
        load.wait()
    stretch_copy = remote(
        stretch, partner_stretch, stretch_sem.at[0], stretch_sem.at[1], {"seq": partner}
    )
    stretch_copy.start()
    for a, src in ((V, v_hbm), (G, g_hbm)):
        @pl.when(onward(a))
        def _():
            z_copy(a, me, src).start()
    for a, src in ((V, v_hbm), (G, g_hbm)):
        p_copy(a, me, src).start()

    squares = sec_sum(0)
    root = lax.rsqrt(squares * (1.0 / width) + EPSILON)
    q_root, k_root = root[0:1], root[1:2]
    kb[me] = (k_wide * as_column(k_root) * k_gain[...]).astype(jnp.bfloat16)
    @pl.when(has_up)
    def _():
        z_copy(K, me).start()
    p_copy(K, me).start()
    qb[me] = (q_wide * as_column(q_root) * q_gain[...]).astype(jnp.bfloat16)
    @pl.when(has_down)
    def _():
        z_copy(Q, me).start()
    p_copy(Q, me).start()
    loads[2].wait()
    loads[3].wait()

    def hidden_bias(key_stretch, query_stretch):
        parts = []
        for at in range(0, rows, FRAME):
            row = jnp.where(key_stretch[:, at : at + 1] <= query_stretch, 0.0, NEG_FILL)
            parts.append(jnp.broadcast_to(row, (FRAME, rows)))
        return jnp.concatenate(parts, axis=0)

    top[...] = jnp.full((1, rows), NEG_FILL, jnp.float32)
    total[...] = jnp.zeros((1, rows), jnp.float32)
    acc[...] = jnp.zeros_like(acc)

    def forward(b, bias=None):
        scores = nt(kb[b], qb[me]) * log2_scale
        if bias is not None:
            scores = scores + bias
        s_buf[b] = scores
        old = top[...]
        new = jnp.maximum(old, jnp.max(scores, axis=0, keepdims=True))
        weights = jnp.exp2(scores - new)
        factor = jnp.exp2(old - new)
        top[...] = new
        total[...] = total[...] * factor + jnp.sum(weights, axis=0, keepdims=True)
        acc[...] = acc[...] * factor + tn(vb[b], weights.astype(jnp.bfloat16))
        dp_buf[b] = nt(vb[b], gb[me])

    def key_scores(b, slot, bias=None):
        scores = nt(kb[me], qb[b]) * log2_scale
        if bias is not None:
            scores = scores + bias
        s_buf[slot] = scores
        dp_buf[slot] = nt(vb[me], gb[b])

    own_stretch = stretch[...]
    forward(me, hidden_bias(own_stretch, own_stretch))

    def stat_copy(b, slot):
        return remote(
            stats.at[slot], stats.at[slot], stat_send.at[b], stat_recv.at[slot], {"seq": b}
        )

    def loop(start, stop, body):
        def run(i, carry):
            body(i)
            return carry
        lax.fori_loop(start, stop, run, 0)

    att_store = pltpu.make_async_copy(att_out, att_hbm, local.at[0])

    def finish_forward():
        attended = (acc[...] / total[...]).astype(jnp.bfloat16).astype(jnp.float32)
        log_total = top[...] + jnp.log2(total[...])
        delta = jnp.sum(gb[me].astype(jnp.float32).T * attended, axis=0, keepdims=True)
        stats[me] = jnp.zeros((8, rows), jnp.float32)
        stats[me, 0:1, :] = log_total
        stats[me, 1:2, :] = delta

        def stat_start(b):
            @pl.when(b != me)
            def _():
                stat_copy(b, me).start()

        loop(0, (level + 1) * span, stat_start)
        att_out[...] = attended.T.astype(jnp.bfloat16)
        att_store.start()
        acc[...] = jnp.zeros_like(acc)

        def query_tail(at):
            pair = pl.ds(at * span, span)
            scores = s_buf[pair].reshape(span * rows, rows)
            chances = jnp.exp2(scores - log_total)
            grads = chances * (dp_buf[pair].reshape(span * rows, rows) - delta)
            acc[...] += tn(kb[pair].reshape(span * rows, d), grads.astype(jnp.bfloat16))

        loop(0, level + 1, query_tail)
        dq = acc[...].T * scale
        dq_out[...] = dq
        sec[1, 0] = jnp.broadcast_to(
            row_sum_of(dq * q_gain[...] * q_raw[...].astype(jnp.float32)), (8, rows)
        )
        sec_start(1)

    dk_acc[...] = jnp.zeros_like(dk_acc)
    dv_acc[...] = jnp.zeros_like(dv_acc)

    def key_level(at):
        key_grad, value_grad = [], []
        for r in range(span):
            b = at * span + r
            @pl.when(b != me)
            def _():
                stat_copy(partner, b).wait_recv()
        for r in range(span):
            b = at * span + r
            slot = jnp.where(b == partner, n, b)
            chances = jnp.exp2(s_buf[slot] - stats[b, 0:1, :])
            value_grad.append(nn(chances.astype(jnp.bfloat16), gb[b]))
            grads = chances * (dp_buf[slot] - stats[b, 1:2, :])
            key_grad.append(nn(grads.astype(jnp.bfloat16), qb[b]))
        dv_acc[...] += sum(value_grad)
        dk_acc[...] += sum(key_grad)

    def step(s, first):
        low, high = me - span * s, me + span * s
        for a in (V, G, K, Q):
            slot = low if a in (V, K) else high
            @pl.when(low >= 0 if a in (V, K) else high < n)
            def _():
                p_copy(a, slot).wait_recv()
                @pl.when(onward(a))
                def _():
                    z_copy(a, slot).start()
                if not first:
                    p_copy(a, slot).start()
        if first:
            for a in (V, G, K, Q):
                p_copy(a, partner).wait_recv()
                @pl.when(onward(a))
                def _():
                    z_copy(a, partner).start()
            stretch_copy.wait_recv()
            other_stretch = partner_stretch[...]
            forward(partner, hidden_bias(other_stretch, own_stretch))
            @pl.when(level == 0)
            def _():
                finish_forward()
            key_scores(partner, n, hidden_bias(own_stretch, other_stretch))
        @pl.when(low >= 0)
        def _():
            forward(low)
        @pl.when(high < n)
        def _():
            key_scores(high, high)
        if not first:
            across(s - 1)
            @pl.when(level == s - 1)
            def _():
                finish_forward()
            @pl.when(level <= s - 2)
            def _():
                key_level(s - 2)

    def across(s):
        low, high = partner - span * s, partner + span * s
        @pl.when(low >= 0)
        def _():
            p_copy(V, low).wait_recv()
            p_copy(K, low).wait_recv()
            forward(low)
        @pl.when(high < n)
        def _():
            p_copy(G, high).wait_recv()
            p_copy(Q, high).wait_recv()
            key_scores(high, high)

    step(1, True)
    loop(2, levels, lambda s: step(s, False))
    across(levels - 1)
    @pl.when(level == levels - 1)
    def _():
        finish_forward()

    loop(jnp.maximum(level, levels - 2), levels, key_level)
    dv_store = pltpu.make_async_copy(dv_acc, dv_hbm, local.at[1])
    dv_store.start()
    dk = dk_acc[...] * scale
    sec[2, 0] = jnp.broadcast_to(row_sum_of(dk * k_gain[...] * k_wide), (8, rows))
    sec_start(2)

    q_part = q_root * q_root * q_root * (sec_sum(1)[0:1] * (1.0 / width))
    dq_out[...] = q_gain[...] * as_column(q_root) * dq_out[...] - q_wide * as_column(q_part)
    dq_store = pltpu.make_async_copy(dq_out, dq_hbm, local.at[2])
    dq_store.start()
    k_part = k_root * k_root * k_root * (sec_sum(2)[0:1] * (1.0 / width))
    dk_out[...] = k_gain[...] * as_column(k_root) * dk - k_wide * as_column(k_part)
    dk_store = pltpu.make_async_copy(dk_out, dk_hbm, local.at[3])
    dk_store.start()

    for phase in range(3):
        for s in range(1, n_sec):
            sec_copy(phase, s).wait_send()
    stretch_copy.wait_send()

    def stat_end(b):
        @pl.when(b != me)
        def _():
            stat_copy(b, me).wait_send()

    loop(0, (level + 1) * span, stat_end)
    for a in range(4):
        p_copy(a, me).wait_send()
        @pl.when(onward(a))
        def _():
            z_copy(a, me).wait_send()
            z_copy(a, partner).wait_send()

        def sent(s):
            slot = me - span * s if a in (V, K) else me + span * s
            @pl.when(slot >= 0 if a in (V, K) else slot < n)
            def _():
                @pl.when(onward(a))
                def _():
                    z_copy(a, slot).wait_send()
                @pl.when(s >= 2)
                def _():
                    p_copy(a, slot).wait_send()

        loop(1, levels, sent)
    att_store.wait()
    dv_store.wait()
    dq_store.wait()
    dk_store.wait()


def store_kernel(*refs):
    sources, targets, sems = refs[:4], refs[4:8], refs[8]
    copies = [
        pltpu.make_async_copy(source, target, sems.at[i])
        for i, (source, target) in enumerate(zip(sources, targets))
    ]
    for copy in copies:
        copy.start()
    for copy in copies:
        copy.wait()


def on_device(n_sec, n, queries, key_rows, values, out_grad, query_gain, key_gain, stretch_id):
    rows, d = queries.shape
    assert rows * 2 == FRAME * GROUP_FRAMES and n % 2 == 0
    f32, bf16 = jnp.float32, jnp.bfloat16
    any_space = pl.BlockSpec(memory_space=pl.ANY)
    hbm = pl.BlockSpec(memory_space=pltpu.HBM)
    dma = pltpu.SemaphoreType.DMA
    block = pltpu.VMEM((n, rows, d), bf16)
    shapes = (jax.ShapeDtypeStruct((rows, d), bf16),) + (jax.ShapeDtypeStruct((rows, d), f32),) * 3
    results = pl.pallas_call(
        functools.partial(kernel, n_sec, n),
        out_shape=shapes,
        in_specs=[hbm] * 7,
        out_specs=(any_space,) * 4,
        scratch_shapes=[
            pltpu.VMEM((rows, d), bf16),
            pltpu.VMEM((rows, d), bf16),
            pltpu.VMEM((1, d), f32),
            pltpu.VMEM((1, d), f32),
            pltpu.VMEM((1, rows), jnp.int32),
            block, block, block, block,
            pltpu.VMEM((1, rows), jnp.int32),
            pltpu.VMEM((3, n_sec, 8, rows), f32),
            pltpu.VMEM((n, 8, rows), f32),
            pltpu.VMEM((n + 1, rows, rows), f32),
            pltpu.VMEM((n + 1, rows, rows), f32),
            pltpu.VMEM((1, rows), f32),
            pltpu.VMEM((1, rows), f32),
            pltpu.VMEM((d, rows), f32),
            pltpu.VMEM((rows, d), f32),
            pltpu.VMEM((rows, d), f32),
            pltpu.VMEM((rows, d), bf16),
            pltpu.VMEM((rows, d), f32),
            pltpu.VMEM((rows, d), f32),
            dma((4, n)),
            dma((4, n)),
            dma((4, n)),
            dma((2,)),
            dma((3, n_sec)),
            dma((3, n_sec)),
            dma((n,)),
            dma((n,)),
            dma((7,)),
        ],
        compiler_params=pltpu.CompilerParams(
            collective_id=0, has_side_effects=True, vmem_limit_bytes=VMEM_BYTES
        ),
        name="stretch_attention",
    )(
        queries, key_rows, values, out_grad,
        query_gain.reshape(1, d), key_gain.reshape(1, d), stretch_id.reshape(1, rows),
    )
    return pl.pallas_call(
        store_kernel,
        out_shape=shapes,
        in_specs=[any_space] * 4,
        out_specs=(hbm,) * 4,
        scratch_shapes=[dma((4,))],
        compiler_params=pltpu.CompilerParams(vmem_limit_bytes=VMEM_BYTES),
        name="store_results",
    )(*results)


def solution(mesh):
    placed = (
        P("seq", "section"),
        P("seq", "section"),
        P("seq", "section"),
        P("seq", "section"),
        P("section"),
        P("section"),
        P("seq"),
    )
    return jax.shard_map(
        functools.partial(on_device, mesh.shape["section"], mesh.shape["seq"]),
        mesh=mesh,
        in_specs=placed,
        out_specs=(P("seq", "section"),) * 4,
        check_vma=False,
    )
```

```python
import functools
import math

import jax
import jax.numpy as jnp
from jax import lax
from jax.experimental import pallas as pl
from jax.experimental.pallas import tpu as pltpu
from jax.sharding import PartitionSpec as P

EPSILON = 1e-06
NEG_FILL = -1e30
FRAME = 128
GROUP_FRAMES = 4
VMEM_BYTES = 60 * 1024 * 1024
V, K, G, Q = range(4)
MESH = pl.DeviceIdType.MESH


def dot(a, b, contract):
    return lax.dot_general(
        a, b, (contract, ((), ())), preferred_element_type=jnp.float32
    )


def nt(a, b):
    return dot(a, b, ((1,), (1,)))


def tn(a, b):
    return dot(a, b, ((0,), (0,)))


def nn(a, b):
    return dot(a, b, ((1,), (0,)))


def kernel(
    n_sec, n,
    q_hbm, k_hbm, v_hbm, g_hbm, q_gain_hbm, k_gain_hbm, stretch_hbm,
    att_hbm, dq_hbm, dk_hbm, dv_hbm,
    q_raw, k_raw, q_gain, k_gain, stretch, vb, kb, gb, qb, partner_stretch, sec, stats, s_buf, dp_buf,
    top, total, acc, dk_acc, dv_acc, att_out, dq_out, dk_out,
    recv, send_z, send_p, stretch_sem, sec_send, sec_recv, stat_send, stat_recv, local,
):
    rows, d = q_raw.shape
    span = 2
    levels = n // span
    width = d * n_sec
    scale = 1.0 / math.sqrt(d)
    log2_scale = scale * math.log2(math.e)
    me = lax.axis_index("seq")
    my_sec = lax.axis_index("section")
    level = me // span
    side = me % span
    partner = me + 1 - 2 * side
    has_up = level < levels - 1
    has_down = level > 0
    bufs = [vb, kb, gb, qb]

    loads = [
        pltpu.make_async_copy(q_hbm, q_raw, local.at[0]),
        pltpu.make_async_copy(k_hbm, k_raw, local.at[1]),
        pltpu.make_async_copy(v_hbm, vb.at[me], local.at[2]),
        pltpu.make_async_copy(g_hbm, gb.at[me], local.at[3]),
        pltpu.make_async_copy(q_gain_hbm, q_gain, local.at[4]),
        pltpu.make_async_copy(k_gain_hbm, k_gain, local.at[5]),
        pltpu.make_async_copy(stretch_hbm, stretch, local.at[6]),
    ]
    for load in loads:
        load.start()

    barrier = pltpu.get_barrier_semaphore()
    for step in range(1, n_sec):
        pl.semaphore_signal(
            barrier, inc=1, device_id={"section": lax.rem(my_sec + step, n_sec)},
            device_id_type=MESH,
        )
    for step in range(1, n):
        pl.semaphore_signal(
            barrier, inc=1, device_id={"seq": lax.rem(me + step, n)}, device_id_type=MESH
        )

    def remote(src, dst, send_sem, recv_sem, device):
        return pltpu.make_async_remote_copy(
            src_ref=src, dst_ref=dst, send_sem=send_sem, recv_sem=recv_sem,
            device_id=device, device_id_type=MESH,
        )

    def z_copy(a, slot, src=None):
        to = me + span if a in (V, K) else me - span
        block = bufs[a].at[slot]
        return remote(
            block if src is None else src, block, send_z.at[a, slot], recv.at[a, slot],
            {"seq": to},
        )

    def p_copy(a, slot, src=None):
        block = bufs[a].at[slot]
        return remote(
            block if src is None else src, block, send_p.at[a, slot], recv.at[a, slot],
            {"seq": partner},
        )

    def onward(a):
        return has_up if a in (V, K) else has_down

    def sec_copy(phase, step):
        return remote(
            sec.at[phase, 0], sec.at[phase, step], sec_send.at[phase, step],
            sec_recv.at[phase, step],
            {"section": lax.rem(my_sec + step, n_sec)},
        )

    def sec_start(phase):
        for step in range(1, n_sec):
            sec_copy(phase, step).start()

    def sec_sum(phase):
        result = sec[phase, 0]
        for step in range(1, n_sec):
            sec_copy(phase, step).wait_recv()
            result = result + sec[phase, step]
        return result

    def row_sum_of(matrix):
        return jnp.sum(matrix.T, axis=0, keepdims=True)

    def as_column(row):
        return jnp.broadcast_to(row, (d, rows)).T

    loads[0].wait()
    loads[1].wait()
    q_wide = q_raw[...].astype(jnp.float32)
    k_wide = k_raw[...].astype(jnp.float32)
    sec[0, 0] = jnp.zeros((8, rows), jnp.float32)
    sec[0, 0, 0:1, :] = row_sum_of(q_wide * q_wide)
    sec[0, 0, 1:2, :] = row_sum_of(k_wide * k_wide)

    pl.semaphore_wait(barrier, n_sec - 1 + n - 1)

    sec_start(0)
    for load in loads[4:]:
        load.wait()
    stretch_copy = remote(
        stretch, partner_stretch, stretch_sem.at[0], stretch_sem.at[1], {"seq": partner}
    )
    stretch_copy.start()
    for a, src in ((V, v_hbm), (G, g_hbm)):
        @pl.when(onward(a))
        def _():
            z_copy(a, me, src).start()
    for a, src in ((V, v_hbm), (G, g_hbm)):
        p_copy(a, me, src).start()

    squares = sec_sum(0)
    root = lax.rsqrt(squares * (1.0 / width) + EPSILON)
    q_root, k_root = root[0:1], root[1:2]
    kb[me] = (k_wide * as_column(k_root) * k_gain[...]).astype(jnp.bfloat16)
    @pl.when(has_up)
    def _():
        z_copy(K, me).start()
    p_copy(K, me).start()
    qb[me] = (q_wide * as_column(q_root) * q_gain[...]).astype(jnp.bfloat16)
    @pl.when(has_down)
    def _():
        z_copy(Q, me).start()
    p_copy(Q, me).start()
    loads[2].wait()
    loads[3].wait()

    def hidden_bias(key_stretch, query_stretch):
        parts = []
        for at in range(0, rows, FRAME):
            row = jnp.where(key_stretch[:, at : at + 1] <= query_stretch, 0.0, NEG_FILL)
            parts.append(jnp.broadcast_to(row, (FRAME, rows)))
        return jnp.concatenate(parts, axis=0)

    top[...] = jnp.full((1, rows), NEG_FILL, jnp.float32)
    total[...] = jnp.zeros((1, rows), jnp.float32)
    acc[...] = jnp.zeros_like(acc)

    def forward(b, bias=None):
        scores = nt(kb[b], qb[me]) * log2_scale
        if bias is not None:
            scores = scores + bias
        s_buf[b] = scores
        old = top[...]
        new = jnp.maximum(old, jnp.max(scores, axis=0, keepdims=True))
        weights = jnp.exp2(scores - new)
        factor = jnp.exp2(old - new)
        top[...] = new
        total[...] = total[...] * factor + jnp.sum(weights, axis=0, keepdims=True)
        acc[...] = acc[...] * factor + tn(vb[b], weights.astype(jnp.bfloat16))

    def key_scores(b, slot, bias=None):
        scores = nt(kb[me], qb[b]) * log2_scale
        if bias is not None:
            scores = scores + bias
        s_buf[slot] = scores
        dp_buf[slot] = nt(vb[me], gb[b])

    own_stretch = stretch[...]
    forward(me, hidden_bias(own_stretch, own_stretch))
    dp_buf[me] = nt(vb[me], gb[me])

    def stat_copy(b, slot):
        return remote(
            stats.at[slot], stats.at[slot], stat_send.at[b], stat_recv.at[slot], {"seq": b}
        )

    def loop(start, stop, body):
        def run(i, carry):
            body(i)
            return carry
        lax.fori_loop(start, stop, run, 0)

    att_store = pltpu.make_async_copy(att_out, att_hbm, local.at[0])

    def finish_forward():
        attended = (acc[...] / total[...]).astype(jnp.bfloat16).astype(jnp.float32)
        log_total = top[...] + jnp.log2(total[...])
        delta = jnp.sum(gb[me].astype(jnp.float32).T * attended, axis=0, keepdims=True)
        stats[me] = jnp.zeros((8, rows), jnp.float32)
        stats[me, 0:1, :] = log_total
        stats[me, 1:2, :] = delta

        def stat_start(b):
            @pl.when(b != me)
            def _():
                stat_copy(b, me).start()

        loop(0, (level + 1) * span, stat_start)
        att_out[...] = attended.T.astype(jnp.bfloat16)
        att_store.start()

    def query_side():
        acc[...] = jnp.zeros_like(acc)
        log_total, delta = stats[me, 0:1, :], stats[me, 1:2, :]

        def query_tail(at):
            pair = pl.ds(at * span, span)
            scores = s_buf[pair].reshape(span * rows, rows)
            chances = jnp.exp2(scores - log_total)
            grads = chances * (nt(vb[pair].reshape(span * rows, d), gb[me]) - delta)
            acc[...] += tn(kb[pair].reshape(span * rows, d), grads.astype(jnp.bfloat16))

        loop(0, level + 1, query_tail)
        dq = acc[...].T * scale
        dq_out[...] = dq
        sec[1, 0] = jnp.broadcast_to(
            row_sum_of(dq * q_gain[...] * q_raw[...].astype(jnp.float32)), (8, rows)
        )
        sec_start(1)

    dk_acc[...] = jnp.zeros_like(dk_acc)
    dv_acc[...] = jnp.zeros_like(dv_acc)

    def key_level(at):
        key_grad, value_grad = [], []
        for r in range(span):
            b = at * span + r
            @pl.when(b != me)
            def _():
                stat_copy(partner, b).wait_recv()
        for r in range(span):
            b = at * span + r
            slot = jnp.where(b == partner, n, b)
            chances = jnp.exp2(s_buf[slot] - stats[b, 0:1, :])
            value_grad.append(nn(chances.astype(jnp.bfloat16), gb[b]))
            grads = chances * (dp_buf[slot] - stats[b, 1:2, :])
            key_grad.append(nn(grads.astype(jnp.bfloat16), qb[b]))
        dv_acc[...] += sum(value_grad)
        dk_acc[...] += sum(key_grad)

    def step(s, first):
        low, high = me - span * s, me + span * s
        for a in (V, G, K, Q):
            slot = low if a in (V, K) else high
            @pl.when(low >= 0 if a in (V, K) else high < n)
            def _():
                p_copy(a, slot).wait_recv()
                @pl.when(onward(a))
                def _():
                    z_copy(a, slot).start()
                if not first:
                    p_copy(a, slot).start()
        if first:
            for a in (V, G, K, Q):
                p_copy(a, partner).wait_recv()
                @pl.when(onward(a))
                def _():
                    z_copy(a, partner).start()
            stretch_copy.wait_recv()
            other_stretch = partner_stretch[...]
            forward(partner, hidden_bias(other_stretch, own_stretch))
            @pl.when(level == 0)
            def _():
                finish_forward()
                query_side()
                key_scores(partner, n, hidden_bias(own_stretch, other_stretch))
        @pl.when(low >= 0)
        def _():
            forward(low)
        @pl.when((high < n) & (level == 0))
        def _():
            key_scores(high, high)
        if not first:
            across(s - 1)
            @pl.when(level == s - 1)
            def _():
                finish_forward()
            @pl.when((level == 0) & (s >= 2))
            def _():
                key_level(s - 2)

    def across(s):
        low, high = partner - span * s, partner + span * s
        @pl.when(low >= 0)
        def _():
            p_copy(V, low).wait_recv()
            p_copy(K, low).wait_recv()
            forward(low)
        @pl.when(high < n)
        def _():
            p_copy(G, high).wait_recv()
            p_copy(Q, high).wait_recv()
            @pl.when(level == 0)
            def _():
                key_scores(high, high)

    step(1, True)
    loop(2, levels, lambda s: step(s, False))
    across(levels - 1)
    @pl.when(level == levels - 1)
    def _():
        finish_forward()

    def key_scores_level(at):
        for r in range(span):
            key_scores(at * span + r, at * span + r)

    @pl.when(level > 0)
    def _():
        query_side()
        other_stretch = partner_stretch[...]
        key_scores(partner, n, hidden_bias(own_stretch, other_stretch))
        loop(level + 1, levels, key_scores_level)

    loop(jnp.where(level == 0, levels - 2, level), levels, key_level)
    dv_store = pltpu.make_async_copy(dv_acc, dv_hbm, local.at[1])
    dv_store.start()
    dk = dk_acc[...] * scale
    sec[2, 0] = jnp.broadcast_to(row_sum_of(dk * k_gain[...] * k_wide), (8, rows))
    sec_start(2)

    q_part = q_root * q_root * q_root * (sec_sum(1)[0:1] * (1.0 / width))
    dq_out[...] = q_gain[...] * as_column(q_root) * dq_out[...] - q_wide * as_column(q_part)
    dq_store = pltpu.make_async_copy(dq_out, dq_hbm, local.at[2])
    dq_store.start()
    k_part = k_root * k_root * k_root * (sec_sum(2)[0:1] * (1.0 / width))
    dk_out[...] = k_gain[...] * as_column(k_root) * dk - k_wide * as_column(k_part)
    dk_store = pltpu.make_async_copy(dk_out, dk_hbm, local.at[3])
    dk_store.start()

    for phase in range(3):
        for s in range(1, n_sec):
            sec_copy(phase, s).wait_send()
    stretch_copy.wait_send()

    def stat_end(b):
        @pl.when(b != me)
        def _():
            stat_copy(b, me).wait_send()

    loop(0, (level + 1) * span, stat_end)
    for a in range(4):
        p_copy(a, me).wait_send()
        @pl.when(onward(a))
        def _():
            z_copy(a, me).wait_send()
            z_copy(a, partner).wait_send()

        def sent(s):
            slot = me - span * s if a in (V, K) else me + span * s
            @pl.when(slot >= 0 if a in (V, K) else slot < n)
            def _():
                @pl.when(onward(a))
                def _():
                    z_copy(a, slot).wait_send()
                @pl.when(s >= 2)
                def _():
                    p_copy(a, slot).wait_send()

        loop(1, levels, sent)
    att_store.wait()
    dv_store.wait()
    dq_store.wait()
    dk_store.wait()


def store_kernel(*refs):
    sources, targets, staged, sems = refs[:4], refs[4:8], refs[8:12], refs[12]
    loads = [pltpu.make_async_copy(sources[i], staged[i], sems.at[0, i]) for i in range(4)]
    stores = [pltpu.make_async_copy(staged[i], targets[i], sems.at[1, i]) for i in range(4)]
    for load in loads:
        load.start()
    for load, store in zip(loads, stores):
        load.wait()
        store.start()
    for store in stores:
        store.wait()


def on_device(n_sec, n, queries, key_rows, values, out_grad, query_gain, key_gain, stretch_id):
    rows, d = queries.shape
    assert rows * 2 == FRAME * GROUP_FRAMES and n % 2 == 0
    f32, bf16 = jnp.float32, jnp.bfloat16
    any_space = pl.BlockSpec(memory_space=pl.ANY)
    hbm = pl.BlockSpec(memory_space=pltpu.HBM)
    dma = pltpu.SemaphoreType.DMA
    block = pltpu.VMEM((n, rows, d), bf16)
    shapes = (jax.ShapeDtypeStruct((rows, d), bf16),) + (jax.ShapeDtypeStruct((rows, d), f32),) * 3
    results = pl.pallas_call(
        functools.partial(kernel, n_sec, n),
        out_shape=shapes,
        in_specs=[hbm] * 7,
        out_specs=(any_space,) * 4,
        scratch_shapes=[
            pltpu.VMEM((rows, d), bf16),
            pltpu.VMEM((rows, d), bf16),
            pltpu.VMEM((1, d), f32),
            pltpu.VMEM((1, d), f32),
            pltpu.VMEM((1, rows), jnp.int32),
            block, block, block, block,
            pltpu.VMEM((1, rows), jnp.int32),
            pltpu.VMEM((3, n_sec, 8, rows), f32),
            pltpu.VMEM((n, 8, rows), f32),
            pltpu.VMEM((n + 1, rows, rows), f32),
            pltpu.VMEM((n + 1, rows, rows), f32),
            pltpu.VMEM((1, rows), f32),
            pltpu.VMEM((1, rows), f32),
            pltpu.VMEM((d, rows), f32),
            pltpu.VMEM((rows, d), f32),
            pltpu.VMEM((rows, d), f32),
            pltpu.VMEM((rows, d), bf16),
            pltpu.VMEM((rows, d), f32),
            pltpu.VMEM((rows, d), f32),
            dma((4, n)),
            dma((4, n)),
            dma((4, n)),
            dma((2,)),
            dma((3, n_sec)),
            dma((3, n_sec)),
            dma((n,)),
            dma((n,)),
            dma((7,)),
        ],
        compiler_params=pltpu.CompilerParams(
            collective_id=0, has_side_effects=True, vmem_limit_bytes=VMEM_BYTES
        ),
        name="stretch_attention",
    )(
        queries, key_rows, values, out_grad,
        query_gain.reshape(1, d), key_gain.reshape(1, d), stretch_id.reshape(1, rows),
    )
    return pl.pallas_call(
        store_kernel,
        out_shape=shapes,
        in_specs=[any_space] * 4,
        out_specs=(hbm,) * 4,
        scratch_shapes=[pltpu.VMEM(shape.shape, shape.dtype) for shape in shapes] + [dma((2, 4))],
        compiler_params=pltpu.CompilerParams(vmem_limit_bytes=VMEM_BYTES),
        name="store_results",
    )(*results)


def solution(mesh):
    placed = (
        P("seq", "section"),
        P("seq", "section"),
        P("seq", "section"),
        P("seq", "section"),
        P("section"),
        P("section"),
        P("seq"),
    )
    return jax.shard_map(
        functools.partial(on_device, mesh.shape["section"], mesh.shape["seq"]),
        mesh=mesh,
        in_specs=placed,
        out_specs=(P("seq", "section"),) * 4,
        check_vma=False,
    )
```

```python
import functools
import math

import jax
import jax.numpy as jnp
from jax import lax
from jax.experimental import pallas as pl
from jax.experimental.pallas import tpu as pltpu
from jax.sharding import PartitionSpec as P

EPSILON = 1e-06
NEG_FILL = -1e30
FRAME = 128
GROUP_FRAMES = 4
VMEM_BYTES = 60 * 1024 * 1024
V, K, G, Q = range(4)
MESH = pl.DeviceIdType.MESH


def dot(a, b, contract):
    return lax.dot_general(
        a, b, (contract, ((), ())), preferred_element_type=jnp.float32
    )


def nt(a, b):
    return dot(a, b, ((1,), (1,)))


def tn(a, b):
    return dot(a, b, ((0,), (0,)))


def nn(a, b):
    return dot(a, b, ((1,), (0,)))


def kernel(
    n_sec, n,
    q_hbm, k_hbm, v_hbm, g_hbm, q_gain_hbm, k_gain_hbm, stretch_hbm,
    att_hbm, dq_hbm, dk_hbm, dv_hbm,
    q_raw, k_raw, q_gain, k_gain, stretch, vb, kb, gb, qb, partner_stretch, sec, stats, s_buf, dp_buf,
    top, total, acc, dk_acc, dv_acc, att_out, dq_out, dk_out,
    recv, send_z, send_p, stretch_sem, sec_send, sec_recv, stat_send, stat_recv, local,
):
    rows, d = q_raw.shape
    span = 2
    levels = n // span
    width = d * n_sec
    scale = 1.0 / math.sqrt(d)
    log2_scale = scale * math.log2(math.e)
    me = lax.axis_index("seq")
    my_sec = lax.axis_index("section")
    level = me // span
    side = me % span
    partner = me + 1 - 2 * side
    has_up = level < levels - 1
    has_down = level > 0
    bufs = [vb, kb, gb, qb]

    loads = [
        pltpu.make_async_copy(q_hbm, q_raw, local.at[0]),
        pltpu.make_async_copy(k_hbm, k_raw, local.at[1]),
        pltpu.make_async_copy(v_hbm, vb.at[me], local.at[2]),
        pltpu.make_async_copy(g_hbm, gb.at[me], local.at[3]),
        pltpu.make_async_copy(q_gain_hbm, q_gain, local.at[4]),
        pltpu.make_async_copy(k_gain_hbm, k_gain, local.at[5]),
        pltpu.make_async_copy(stretch_hbm, stretch, local.at[6]),
    ]
    for load in loads:
        load.start()

    barrier = pltpu.get_barrier_semaphore()
    for step in range(1, n_sec):
        pl.semaphore_signal(
            barrier, inc=1, device_id={"section": lax.rem(my_sec + step, n_sec)},
            device_id_type=MESH,
        )
    for step in range(1, n):
        pl.semaphore_signal(
            barrier, inc=1, device_id={"seq": lax.rem(me + step, n)}, device_id_type=MESH
        )

    def remote(src, dst, send_sem, recv_sem, device):
        return pltpu.make_async_remote_copy(
            src_ref=src, dst_ref=dst, send_sem=send_sem, recv_sem=recv_sem,
            device_id=device, device_id_type=MESH,
        )

    def z_copy(a, slot, src=None):
        to = me + span if a in (V, K) else me - span
        block = bufs[a].at[slot]
        return remote(
            block if src is None else src, block, send_z.at[a, slot], recv.at[a, slot],
            {"seq": to},
        )

    def p_copy(a, slot, src=None):
        block = bufs[a].at[slot]
        return remote(
            block if src is None else src, block, send_p.at[a, slot], recv.at[a, slot],
            {"seq": partner},
        )

    def onward(a):
        return has_up if a in (V, K) else has_down

    def sec_copy(phase, step):
        return remote(
            sec.at[phase, 0], sec.at[phase, step], sec_send.at[phase, step],
            sec_recv.at[phase, step],
            {"section": lax.rem(my_sec + step, n_sec)},
        )

    def sec_start(phase):
        for step in range(1, n_sec):
            sec_copy(phase, step).start()

    def sec_sum(phase):
        result = sec[phase, 0]
        for step in range(1, n_sec):
            sec_copy(phase, step).wait_recv()
            result = result + sec[phase, step]
        return result

    def row_sum_of(matrix):
        return jnp.sum(matrix.T, axis=0, keepdims=True)

    def as_column(row):
        return jnp.broadcast_to(row, (d, rows)).T

    loads[0].wait()
    loads[1].wait()
    q_wide = q_raw[...].astype(jnp.float32)
    k_wide = k_raw[...].astype(jnp.float32)
    sec[0, 0] = jnp.zeros((8, rows), jnp.float32)
    sec[0, 0, 0:1, :] = row_sum_of(q_wide * q_wide)
    sec[0, 0, 1:2, :] = row_sum_of(k_wide * k_wide)

    pl.semaphore_wait(barrier, n_sec - 1 + n - 1)

    sec_start(0)
    for load in loads[4:]:
        load.wait()
    stretch_copy = remote(
        stretch, partner_stretch, stretch_sem.at[0], stretch_sem.at[1], {"seq": partner}
    )
    stretch_copy.start()
    for a, src in ((V, v_hbm), (G, g_hbm)):
        @pl.when(onward(a))
        def _():
            z_copy(a, me, src).start()
    for a, src in ((V, v_hbm), (G, g_hbm)):
        p_copy(a, me, src).start()

    squares = sec_sum(0)
    root = lax.rsqrt(squares * (1.0 / width) + EPSILON)
    q_root, k_root = root[0:1], root[1:2]
    kb[me] = (k_wide * as_column(k_root) * k_gain[...]).astype(jnp.bfloat16)
    @pl.when(has_up)
    def _():
        z_copy(K, me).start()
    p_copy(K, me).start()
    qb[me] = (q_wide * as_column(q_root) * q_gain[...]).astype(jnp.bfloat16)
    @pl.when(has_down)
    def _():
        z_copy(Q, me).start()
    p_copy(Q, me).start()
    loads[2].wait()
    loads[3].wait()

    def hidden_bias(key_stretch, query_stretch):
        parts = []
        for at in range(0, rows, FRAME):
            row = jnp.where(key_stretch[:, at : at + 1] <= query_stretch, 0.0, NEG_FILL)
            parts.append(jnp.broadcast_to(row, (FRAME, rows)))
        return jnp.concatenate(parts, axis=0)

    top[...] = jnp.full((1, rows), NEG_FILL, jnp.float32)
    total[...] = jnp.zeros((1, rows), jnp.float32)
    acc[...] = jnp.zeros_like(acc)

    def forward(b, bias=None):
        scores = nt(kb[b], qb[me]) * log2_scale
        if bias is not None:
            scores = scores + bias
        s_buf[b] = scores
        old = top[...]
        new = jnp.maximum(old, jnp.max(scores, axis=0, keepdims=True))
        weights = jnp.exp2(scores - new)
        factor = jnp.exp2(old - new)
        top[...] = new
        total[...] = total[...] * factor + jnp.sum(weights, axis=0, keepdims=True)
        acc[...] = acc[...] * factor + tn(vb[b], weights.astype(jnp.bfloat16))

    def key_scores(b, slot, bias=None):
        scores = nt(kb[me], qb[b]) * log2_scale
        if bias is not None:
            scores = scores + bias
        s_buf[slot] = scores
        dp_buf[slot] = nt(vb[me], gb[b])

    own_stretch = stretch[...]
    forward(me, hidden_bias(own_stretch, own_stretch))
    dp_buf[me] = nt(vb[me], gb[me])

    def stat_copy(b, slot):
        return remote(
            stats.at[slot], stats.at[slot], stat_send.at[b], stat_recv.at[slot], {"seq": b}
        )

    def loop(start, stop, body):
        def run(i, carry):
            body(i)
            return carry
        lax.fori_loop(start, stop, run, 0)

    att_store = pltpu.make_async_copy(att_out, att_hbm, local.at[0])

    def finish_forward():
        attended = (acc[...] / total[...]).astype(jnp.bfloat16).astype(jnp.float32)
        log_total = top[...] + jnp.log2(total[...])
        delta = jnp.sum(gb[me].astype(jnp.float32).T * attended, axis=0, keepdims=True)
        stats[me] = jnp.zeros((8, rows), jnp.float32)
        stats[me, 0:1, :] = log_total
        stats[me, 1:2, :] = delta

        def stat_start(b):
            @pl.when(b != me)
            def _():
                stat_copy(b, me).start()

        loop(0, (level + 1) * span, stat_start)
        att_out[...] = attended.T.astype(jnp.bfloat16)
        att_store.start()

    def query_side():
        acc[...] = jnp.zeros_like(acc)
        log_total, delta = stats[me, 0:1, :], stats[me, 1:2, :]

        def query_tail(at):
            pair = pl.ds(at * span, span)
            scores = s_buf[pair].reshape(span * rows, rows)
            chances = jnp.exp2(scores - log_total)
            grads = chances * (nt(vb[pair].reshape(span * rows, d), gb[me]) - delta)
            acc[...] += tn(kb[pair].reshape(span * rows, d), grads.astype(jnp.bfloat16))

        loop(0, level + 1, query_tail)
        dq = acc[...].T * scale
        dq_out[...] = dq
        sec[1, 0] = jnp.broadcast_to(
            row_sum_of(dq * q_gain[...] * q_raw[...].astype(jnp.float32)), (8, rows)
        )
        sec_start(1)

    dk_acc[...] = jnp.zeros_like(dk_acc)
    dv_acc[...] = jnp.zeros_like(dv_acc)

    def key_level(at):
        key_grad, value_grad = [], []
        for r in range(span):
            b = at * span + r
            @pl.when(b != me)
            def _():
                stat_copy(partner, b).wait_recv()
        for r in range(span):
            b = at * span + r
            slot = jnp.where(b == partner, n, b)
            chances = jnp.exp2(s_buf[slot] - stats[b, 0:1, :])
            value_grad.append(nn(chances.astype(jnp.bfloat16), gb[b]))
            grads = chances * (dp_buf[slot] - stats[b, 1:2, :])
            key_grad.append(nn(grads.astype(jnp.bfloat16), qb[b]))
        dv_acc[...] += sum(value_grad)
        dk_acc[...] += sum(key_grad)

    def step(s, first):
        low, high = me - span * s, me + span * s
        for a in (V, G, K, Q):
            slot = low if a in (V, K) else high
            @pl.when(low >= 0 if a in (V, K) else high < n)
            def _():
                p_copy(a, slot).wait_recv()
                @pl.when(onward(a))
                def _():
                    z_copy(a, slot).start()
                if not first:
                    p_copy(a, slot).start()
            if not first:
                @pl.when((s == 2) & onward(a))
                def _():
                    z_copy(a, partner).start()
        if first:
            for a in (V, G, K, Q):
                p_copy(a, partner).wait_recv()
                if levels == 2:
                    @pl.when(onward(a))
                    def _():
                        z_copy(a, partner).start()
            stretch_copy.wait_recv()
            other_stretch = partner_stretch[...]
            forward(partner, hidden_bias(other_stretch, own_stretch))
            @pl.when(level == 0)
            def _():
                finish_forward()
                query_side()
                key_scores(partner, n, hidden_bias(own_stretch, other_stretch))
        @pl.when(low >= 0)
        def _():
            forward(low)
        @pl.when((high < n) & (level == 0))
        def _():
            key_scores(high, high)
        if not first:
            across(s - 1)
            @pl.when(level == s - 1)
            def _():
                finish_forward()
            @pl.when((level == 0) & (s >= 2))
            def _():
                key_level(s - 2)

    def across(s):
        low, high = partner - span * s, partner + span * s
        @pl.when(low >= 0)
        def _():
            p_copy(V, low).wait_recv()
            p_copy(K, low).wait_recv()
            forward(low)
        @pl.when(high < n)
        def _():
            p_copy(G, high).wait_recv()
            p_copy(Q, high).wait_recv()
            @pl.when(level == 0)
            def _():
                key_scores(high, high)

    step(1, True)
    loop(2, levels, lambda s: step(s, False))
    across(levels - 1)
    @pl.when(level == levels - 1)
    def _():
        finish_forward()

    def key_scores_level(at):
        for r in range(span):
            key_scores(at * span + r, at * span + r)

    @pl.when(level > 0)
    def _():
        query_side()
        other_stretch = partner_stretch[...]
        key_scores(partner, n, hidden_bias(own_stretch, other_stretch))
        loop(level + 1, levels, key_scores_level)

    loop(jnp.where(level == 0, levels - 2, level), levels, key_level)
    dv_store = pltpu.make_async_copy(dv_acc, dv_hbm, local.at[1])
    dv_store.start()
    dk = dk_acc[...] * scale
    sec[2, 0] = jnp.broadcast_to(row_sum_of(dk * k_gain[...] * k_wide), (8, rows))
    sec_start(2)

    q_part = q_root * q_root * q_root * (sec_sum(1)[0:1] * (1.0 / width))
    dq_out[...] = q_gain[...] * as_column(q_root) * dq_out[...] - q_wide * as_column(q_part)
    dq_store = pltpu.make_async_copy(dq_out, dq_hbm, local.at[2])
    dq_store.start()
    k_part = k_root * k_root * k_root * (sec_sum(2)[0:1] * (1.0 / width))
    dk_out[...] = k_gain[...] * as_column(k_root) * dk - k_wide * as_column(k_part)
    dk_store = pltpu.make_async_copy(dk_out, dk_hbm, local.at[3])
    dk_store.start()

    for phase in range(3):
        for s in range(1, n_sec):
            sec_copy(phase, s).wait_send()
    stretch_copy.wait_send()

    def stat_end(b):
        @pl.when(b != me)
        def _():
            stat_copy(b, me).wait_send()

    loop(0, (level + 1) * span, stat_end)
    for a in range(4):
        p_copy(a, me).wait_send()
        @pl.when(onward(a))
        def _():
            z_copy(a, me).wait_send()
            z_copy(a, partner).wait_send()

        def sent(s):
            slot = me - span * s if a in (V, K) else me + span * s
            @pl.when(slot >= 0 if a in (V, K) else slot < n)
            def _():
                @pl.when(onward(a))
                def _():
                    z_copy(a, slot).wait_send()
                @pl.when(s >= 2)
                def _():
                    p_copy(a, slot).wait_send()

        loop(1, levels, sent)
    att_store.wait()
    dv_store.wait()
    dq_store.wait()
    dk_store.wait()


def store_kernel(*refs):
    sources, targets, staged, sems = refs[:4], refs[4:8], refs[8:12], refs[12]
    loads = [pltpu.make_async_copy(sources[i], staged[i], sems.at[0, i]) for i in range(4)]
    stores = [pltpu.make_async_copy(staged[i], targets[i], sems.at[1, i]) for i in range(4)]
    for load in loads:
        load.start()
    for load, store in zip(loads, stores):
        load.wait()
        store.start()
    for store in stores:
        store.wait()


def on_device(n_sec, n, queries, key_rows, values, out_grad, query_gain, key_gain, stretch_id):
    rows, d = queries.shape
    assert rows * 2 == FRAME * GROUP_FRAMES and n % 2 == 0
    f32, bf16 = jnp.float32, jnp.bfloat16
    any_space = pl.BlockSpec(memory_space=pl.ANY)
    hbm = pl.BlockSpec(memory_space=pltpu.HBM)
    dma = pltpu.SemaphoreType.DMA
    block = pltpu.VMEM((n, rows, d), bf16)
    shapes = (jax.ShapeDtypeStruct((rows, d), bf16),) + (jax.ShapeDtypeStruct((rows, d), f32),) * 3
    results = pl.pallas_call(
        functools.partial(kernel, n_sec, n),
        out_shape=shapes,
        in_specs=[hbm] * 7,
        out_specs=(any_space,) * 4,
        scratch_shapes=[
            pltpu.VMEM((rows, d), bf16),
            pltpu.VMEM((rows, d), bf16),
            pltpu.VMEM((1, d), f32),
            pltpu.VMEM((1, d), f32),
            pltpu.VMEM((1, rows), jnp.int32),
            block, block, block, block,
            pltpu.VMEM((1, rows), jnp.int32),
            pltpu.VMEM((3, n_sec, 8, rows), f32),
            pltpu.VMEM((n, 8, rows), f32),
            pltpu.VMEM((n + 1, rows, rows), f32),
            pltpu.VMEM((n + 1, rows, rows), f32),
            pltpu.VMEM((1, rows), f32),
            pltpu.VMEM((1, rows), f32),
            pltpu.VMEM((d, rows), f32),
            pltpu.VMEM((rows, d), f32),
            pltpu.VMEM((rows, d), f32),
            pltpu.VMEM((rows, d), bf16),
            pltpu.VMEM((rows, d), f32),
            pltpu.VMEM((rows, d), f32),
            dma((4, n)),
            dma((4, n)),
            dma((4, n)),
            dma((2,)),
            dma((3, n_sec)),
            dma((3, n_sec)),
            dma((n,)),
            dma((n,)),
            dma((7,)),
        ],
        compiler_params=pltpu.CompilerParams(
            collective_id=0, has_side_effects=True, vmem_limit_bytes=VMEM_BYTES
        ),
        name="stretch_attention",
    )(
        queries, key_rows, values, out_grad,
        query_gain.reshape(1, d), key_gain.reshape(1, d), stretch_id.reshape(1, rows),
    )
    return pl.pallas_call(
        store_kernel,
        out_shape=shapes,
        in_specs=[any_space] * 4,
        out_specs=(hbm,) * 4,
        scratch_shapes=[pltpu.VMEM(shape.shape, shape.dtype) for shape in shapes] + [dma((2, 4))],
        compiler_params=pltpu.CompilerParams(vmem_limit_bytes=VMEM_BYTES),
        name="store_results",
    )(*results)


def solution(mesh):
    placed = (
        P("seq", "section"),
        P("seq", "section"),
        P("seq", "section"),
        P("seq", "section"),
        P("section"),
        P("section"),
        P("seq"),
    )
    return jax.shard_map(
        functools.partial(on_device, mesh.shape["section"], mesh.shape["seq"]),
        mesh=mesh,
        in_specs=placed,
        out_specs=(P("seq", "section"),) * 4,
        check_vma=False,
    )
```

```python
import functools
import math

import jax
import jax.numpy as jnp
from jax import lax
from jax.experimental import pallas as pl
from jax.experimental.pallas import tpu as pltpu
from jax.sharding import PartitionSpec as P

EPSILON = 1e-06
NEG_FILL = -1e30
FRAME = 128
GROUP_FRAMES = 4
FAR = 3
VMEM_BYTES = 60 * 1024 * 1024
V, K, G, Q = range(4)
MESH = pl.DeviceIdType.MESH


def dot(a, b, contract):
    return lax.dot_general(
        a, b, (contract, ((), ())), preferred_element_type=jnp.float32
    )


def nt(a, b):
    return dot(a, b, ((1,), (1,)))


def tn(a, b):
    return dot(a, b, ((0,), (0,)))


def nn(a, b):
    return dot(a, b, ((1,), (0,)))


def kernel(
    n_sec, n,
    q_hbm, k_hbm, v_hbm, g_hbm, q_gain_hbm, k_gain_hbm, stretch_hbm,
    att_hbm, dq_hbm, dk_hbm, dv_hbm,
    q_raw, k_raw, q_gain, k_gain, stretch, vb, kb, gb, qb, partner_stretch, sec, stats, s_buf, dp_buf,
    top, total, acc, dk_acc, dv_acc, att_out, dq_out, dk_out,
    recv, send_z, send_p, send_far, stretch_sem, sec_send, sec_recv, stat_send, stat_recv, local,
):
    rows, d = q_raw.shape
    span = 2
    levels = n // span
    width = d * n_sec
    scale = 1.0 / math.sqrt(d)
    log2_scale = scale * math.log2(math.e)
    me = lax.axis_index("seq")
    my_sec = lax.axis_index("section")
    level = me // span
    side = me % span
    partner = me + 1 - 2 * side
    has_up = level < levels - 1
    has_down = level > 0
    bufs = [vb, kb, gb, qb]

    loads = [
        pltpu.make_async_copy(q_hbm, q_raw, local.at[0]),
        pltpu.make_async_copy(k_hbm, k_raw, local.at[1]),
        pltpu.make_async_copy(v_hbm, vb.at[me], local.at[2]),
        pltpu.make_async_copy(g_hbm, gb.at[me], local.at[3]),
        pltpu.make_async_copy(q_gain_hbm, q_gain, local.at[4]),
        pltpu.make_async_copy(k_gain_hbm, k_gain, local.at[5]),
        pltpu.make_async_copy(stretch_hbm, stretch, local.at[6]),
    ]
    for load in loads:
        load.start()

    barrier = pltpu.get_barrier_semaphore()
    for step in range(1, n_sec):
        pl.semaphore_signal(
            barrier, inc=1, device_id={"section": lax.rem(my_sec + step, n_sec)},
            device_id_type=MESH,
        )
    for step in range(1, n):
        pl.semaphore_signal(
            barrier, inc=1, device_id={"seq": lax.rem(me + step, n)}, device_id_type=MESH
        )

    def remote(src, dst, send_sem, recv_sem, device):
        return pltpu.make_async_remote_copy(
            src_ref=src, dst_ref=dst, send_sem=send_sem, recv_sem=recv_sem,
            device_id=device, device_id_type=MESH,
        )

    def z_copy(a, slot, src=None):
        to = me + span if a in (V, K) else me - span
        block = bufs[a].at[slot]
        return remote(
            block if src is None else src, block, send_z.at[a, slot], recv.at[a, slot],
            {"seq": to},
        )

    def p_copy(a, slot, src=None):
        block = bufs[a].at[slot]
        return remote(
            block if src is None else src, block, send_p.at[a, slot], recv.at[a, slot],
            {"seq": partner},
        )

    def far_copy(a, src=None):
        block = bufs[a].at[me]
        to = me + FAR * span if a in (V, K) else me - FAR * span
        return remote(
            block if src is None else src, block, send_far.at[a], recv.at[a, me], {"seq": to}
        )

    def far(a):
        return level + FAR < levels if a in (V, K) else level >= FAR

    def onward(a):
        return has_up if a in (V, K) else has_down

    def sec_copy(phase, step):
        return remote(
            sec.at[phase, 0], sec.at[phase, step], sec_send.at[phase, step],
            sec_recv.at[phase, step],
            {"section": lax.rem(my_sec + step, n_sec)},
        )

    def sec_start(phase):
        for step in range(1, n_sec):
            sec_copy(phase, step).start()

    def sec_sum(phase):
        result = sec[phase, 0]
        for step in range(1, n_sec):
            sec_copy(phase, step).wait_recv()
            result = result + sec[phase, step]
        return result

    def row_sum_of(matrix):
        return jnp.sum(matrix.T, axis=0, keepdims=True)

    def as_column(row):
        return jnp.broadcast_to(row, (d, rows)).T

    loads[0].wait()
    loads[1].wait()
    q_wide = q_raw[...].astype(jnp.float32)
    k_wide = k_raw[...].astype(jnp.float32)
    sec[0, 0] = jnp.zeros((8, rows), jnp.float32)
    sec[0, 0, 0:1, :] = row_sum_of(q_wide * q_wide)
    sec[0, 0, 1:2, :] = row_sum_of(k_wide * k_wide)

    pl.semaphore_wait(barrier, n_sec - 1 + n - 1)

    sec_start(0)
    for load in loads[4:]:
        load.wait()
    stretch_copy = remote(
        stretch, partner_stretch, stretch_sem.at[0], stretch_sem.at[1], {"seq": partner}
    )
    stretch_copy.start()
    for a, src in ((V, v_hbm), (G, g_hbm)):
        @pl.when(far(a))
        def _():
            far_copy(a, src).start()
        @pl.when(onward(a))
        def _():
            z_copy(a, me, src).start()
    for a, src in ((V, v_hbm), (G, g_hbm)):
        p_copy(a, me, src).start()

    squares = sec_sum(0)
    root = lax.rsqrt(squares * (1.0 / width) + EPSILON)
    q_root, k_root = root[0:1], root[1:2]
    kb[me] = (k_wide * as_column(k_root) * k_gain[...]).astype(jnp.bfloat16)
    @pl.when(far(K))
    def _():
        far_copy(K).start()
    @pl.when(has_up)
    def _():
        z_copy(K, me).start()
    p_copy(K, me).start()
    qb[me] = (q_wide * as_column(q_root) * q_gain[...]).astype(jnp.bfloat16)
    @pl.when(far(Q))
    def _():
        far_copy(Q).start()
    @pl.when(has_down)
    def _():
        z_copy(Q, me).start()
    p_copy(Q, me).start()
    loads[2].wait()
    loads[3].wait()

    def hidden_bias(key_stretch, query_stretch):
        parts = []
        for at in range(0, rows, FRAME):
            row = jnp.where(key_stretch[:, at : at + 1] <= query_stretch, 0.0, NEG_FILL)
            parts.append(jnp.broadcast_to(row, (FRAME, rows)))
        return jnp.concatenate(parts, axis=0)

    top[...] = jnp.full((1, rows), NEG_FILL, jnp.float32)
    total[...] = jnp.zeros((1, rows), jnp.float32)
    acc[...] = jnp.zeros_like(acc)

    def forward(b, bias=None):
        scores = nt(kb[b], qb[me]) * log2_scale
        if bias is not None:
            scores = scores + bias
        s_buf[b] = scores
        old = top[...]
        new = jnp.maximum(old, jnp.max(scores, axis=0, keepdims=True))
        weights = jnp.exp2(scores - new)
        factor = jnp.exp2(old - new)
        top[...] = new
        total[...] = total[...] * factor + jnp.sum(weights, axis=0, keepdims=True)
        acc[...] = acc[...] * factor + tn(vb[b], weights.astype(jnp.bfloat16))

    def key_scores(b, slot, bias=None):
        scores = nt(kb[me], qb[b]) * log2_scale
        if bias is not None:
            scores = scores + bias
        s_buf[slot] = scores
        dp_buf[slot] = nt(vb[me], gb[b])

    own_stretch = stretch[...]
    forward(me, hidden_bias(own_stretch, own_stretch))
    dp_buf[me] = nt(vb[me], gb[me])

    def stat_copy(b, slot):
        return remote(
            stats.at[slot], stats.at[slot], stat_send.at[b], stat_recv.at[slot], {"seq": b}
        )

    def loop(start, stop, body):
        def run(i, carry):
            body(i)
            return carry
        lax.fori_loop(start, stop, run, 0)

    att_store = pltpu.make_async_copy(att_out, att_hbm, local.at[0])

    def finish_forward():
        attended = (acc[...] / total[...]).astype(jnp.bfloat16).astype(jnp.float32)
        log_total = top[...] + jnp.log2(total[...])
        delta = jnp.sum(gb[me].astype(jnp.float32).T * attended, axis=0, keepdims=True)
        stats[me] = jnp.zeros((8, rows), jnp.float32)
        stats[me, 0:1, :] = log_total
        stats[me, 1:2, :] = delta

        def stat_start(b):
            @pl.when(b != me)
            def _():
                stat_copy(b, me).start()

        loop(0, (level + 1) * span, stat_start)
        att_out[...] = attended.T.astype(jnp.bfloat16)
        att_store.start()

    def query_side():
        acc[...] = jnp.zeros_like(acc)
        log_total, delta = stats[me, 0:1, :], stats[me, 1:2, :]

        def query_tail(at):
            pair = pl.ds(at * span, span)
            scores = s_buf[pair].reshape(span * rows, rows)
            chances = jnp.exp2(scores - log_total)
            grads = chances * (nt(vb[pair].reshape(span * rows, d), gb[me]) - delta)
            acc[...] += tn(kb[pair].reshape(span * rows, d), grads.astype(jnp.bfloat16))

        loop(0, level + 1, query_tail)
        dq = acc[...].T * scale
        dq_out[...] = dq
        sec[1, 0] = jnp.broadcast_to(
            row_sum_of(dq * q_gain[...] * q_raw[...].astype(jnp.float32)), (8, rows)
        )
        sec_start(1)

    dk_acc[...] = jnp.zeros_like(dk_acc)
    dv_acc[...] = jnp.zeros_like(dv_acc)

    def key_level(at):
        key_grad, value_grad = [], []
        for r in range(span):
            b = at * span + r
            @pl.when(b != me)
            def _():
                stat_copy(partner, b).wait_recv()
        for r in range(span):
            b = at * span + r
            slot = jnp.where(b == partner, n, b)
            chances = jnp.exp2(s_buf[slot] - stats[b, 0:1, :])
            value_grad.append(nn(chances.astype(jnp.bfloat16), gb[b]))
            grads = chances * (dp_buf[slot] - stats[b, 1:2, :])
            key_grad.append(nn(grads.astype(jnp.bfloat16), qb[b]))
        dv_acc[...] += sum(value_grad)
        dk_acc[...] += sum(key_grad)

    def distance(i):
        if levels <= FAR:
            return i
        return jnp.where(i == FAR - 1, FAR, jnp.where(i == FAR, FAR - 1, i))

    def finished_at(i):
        if levels <= FAR:
            return level == i
        late = (i == FAR) & (level == FAR - 1)
        return ((i != FAR - 1) & (level == i)) | late

    def step(i, first):
        s = 1 if first else distance(i)
        low, high = me - span * s, me + span * s
        for a in (V, G, K, Q):
            slot = low if a in (V, K) else high
            @pl.when(low >= 0 if a in (V, K) else high < n)
            def _():
                p_copy(a, slot).wait_recv()
                @pl.when(onward(a) & (s != FAR - 1))
                def _():
                    z_copy(a, slot).start()
                if not first:
                    p_copy(a, slot).start()
        if first:
            for a in (V, G, K, Q):
                p_copy(a, partner).wait_recv()
                @pl.when(onward(a))
                def _():
                    z_copy(a, partner).start()
            stretch_copy.wait_recv()
            other_stretch = partner_stretch[...]
            forward(partner, hidden_bias(other_stretch, own_stretch))
            @pl.when(level == 0)
            def _():
                finish_forward()
                query_side()
                key_scores(partner, n, hidden_bias(own_stretch, other_stretch))
        @pl.when(low >= 0)
        def _():
            forward(low)
        @pl.when((high < n) & (level == 0))
        def _():
            key_scores(high, high)
        if not first:
            across(distance(i - 1))
            @pl.when(finished_at(i - 1))
            def _():
                finish_forward()
            @pl.when(level == 0)
            def _():
                key_level(i - 2)

    def across(s):
        low, high = partner - span * s, partner + span * s
        @pl.when(low >= 0)
        def _():
            p_copy(V, low).wait_recv()
            p_copy(K, low).wait_recv()
            forward(low)
        @pl.when(high < n)
        def _():
            p_copy(G, high).wait_recv()
            p_copy(Q, high).wait_recv()
            @pl.when(level == 0)
            def _():
                key_scores(high, high)

    step(1, True)
    loop(2, levels, lambda i: step(i, False))
    across(distance(levels - 1))
    @pl.when(finished_at(levels - 1))
    def _():
        finish_forward()

    def key_scores_level(at):
        for r in range(span):
            key_scores(at * span + r, at * span + r)

    @pl.when(level > 0)
    def _():
        query_side()
        other_stretch = partner_stretch[...]
        key_scores(partner, n, hidden_bias(own_stretch, other_stretch))
        loop(level + 1, levels, key_scores_level)

    loop(jnp.where(level == 0, levels - 2, level), levels, key_level)
    dv_store = pltpu.make_async_copy(dv_acc, dv_hbm, local.at[1])
    dv_store.start()
    dk = dk_acc[...] * scale
    sec[2, 0] = jnp.broadcast_to(row_sum_of(dk * k_gain[...] * k_wide), (8, rows))
    sec_start(2)

    q_part = q_root * q_root * q_root * (sec_sum(1)[0:1] * (1.0 / width))
    dq_out[...] = q_gain[...] * as_column(q_root) * dq_out[...] - q_wide * as_column(q_part)
    dq_store = pltpu.make_async_copy(dq_out, dq_hbm, local.at[2])
    dq_store.start()
    k_part = k_root * k_root * k_root * (sec_sum(2)[0:1] * (1.0 / width))
    dk_out[...] = k_gain[...] * as_column(k_root) * dk - k_wide * as_column(k_part)
    dk_store = pltpu.make_async_copy(dk_out, dk_hbm, local.at[3])
    dk_store.start()

    for phase in range(3):
        for s in range(1, n_sec):
            sec_copy(phase, s).wait_send()
    stretch_copy.wait_send()

    def stat_end(b):
        @pl.when(b != me)
        def _():
            stat_copy(b, me).wait_send()

    loop(0, (level + 1) * span, stat_end)
    for a in range(4):
        p_copy(a, me).wait_send()
        @pl.when(onward(a))
        def _():
            z_copy(a, me).wait_send()
            z_copy(a, partner).wait_send()
        @pl.when(far(a))
        def _():
            far_copy(a).wait_send()

        def sent(s):
            slot = me - span * s if a in (V, K) else me + span * s
            @pl.when(slot >= 0 if a in (V, K) else slot < n)
            def _():
                @pl.when(onward(a) & (s != FAR - 1))
                def _():
                    z_copy(a, slot).wait_send()
                @pl.when(s >= 2)
                def _():
                    p_copy(a, slot).wait_send()

        loop(1, levels, sent)
    att_store.wait()
    dv_store.wait()
    dq_store.wait()
    dk_store.wait()


def store_kernel(*refs):
    sources, targets, staged, sems = refs[:4], refs[4:8], refs[8:12], refs[12]
    loads = [pltpu.make_async_copy(sources[i], staged[i], sems.at[0, i]) for i in range(4)]
    stores = [pltpu.make_async_copy(staged[i], targets[i], sems.at[1, i]) for i in range(4)]
    for load in loads:
        load.start()
    for load, store in zip(loads, stores):
        load.wait()
        store.start()
    for store in stores:
        store.wait()


def on_device(n_sec, n, queries, key_rows, values, out_grad, query_gain, key_gain, stretch_id):
    rows, d = queries.shape
    assert rows * 2 == FRAME * GROUP_FRAMES and n % 2 == 0
    f32, bf16 = jnp.float32, jnp.bfloat16
    any_space = pl.BlockSpec(memory_space=pl.ANY)
    hbm = pl.BlockSpec(memory_space=pltpu.HBM)
    dma = pltpu.SemaphoreType.DMA
    block = pltpu.VMEM((n, rows, d), bf16)
    shapes = (jax.ShapeDtypeStruct((rows, d), bf16),) + (jax.ShapeDtypeStruct((rows, d), f32),) * 3
    results = pl.pallas_call(
        functools.partial(kernel, n_sec, n),
        out_shape=shapes,
        in_specs=[hbm] * 7,
        out_specs=(any_space,) * 4,
        scratch_shapes=[
            pltpu.VMEM((rows, d), bf16),
            pltpu.VMEM((rows, d), bf16),
            pltpu.VMEM((1, d), f32),
            pltpu.VMEM((1, d), f32),
            pltpu.VMEM((1, rows), jnp.int32),
            block, block, block, block,
            pltpu.VMEM((1, rows), jnp.int32),
            pltpu.VMEM((3, n_sec, 8, rows), f32),
            pltpu.VMEM((n, 8, rows), f32),
            pltpu.VMEM((n + 1, rows, rows), f32),
            pltpu.VMEM((n + 1, rows, rows), f32),
            pltpu.VMEM((1, rows), f32),
            pltpu.VMEM((1, rows), f32),
            pltpu.VMEM((d, rows), f32),
            pltpu.VMEM((rows, d), f32),
            pltpu.VMEM((rows, d), f32),
            pltpu.VMEM((rows, d), bf16),
            pltpu.VMEM((rows, d), f32),
            pltpu.VMEM((rows, d), f32),
            dma((4, n)),
            dma((4, n)),
            dma((4, n)),
            dma((4,)),
            dma((2,)),
            dma((3, n_sec)),
            dma((3, n_sec)),
            dma((n,)),
            dma((n,)),
            dma((7,)),
        ],
        compiler_params=pltpu.CompilerParams(
            collective_id=0, has_side_effects=True, vmem_limit_bytes=VMEM_BYTES
        ),
        name="stretch_attention",
    )(
        queries, key_rows, values, out_grad,
        query_gain.reshape(1, d), key_gain.reshape(1, d), stretch_id.reshape(1, rows),
    )
    return pl.pallas_call(
        store_kernel,
        out_shape=shapes,
        in_specs=[any_space] * 4,
        out_specs=(hbm,) * 4,
        scratch_shapes=[pltpu.VMEM(shape.shape, shape.dtype) for shape in shapes] + [dma((2, 4))],
        compiler_params=pltpu.CompilerParams(vmem_limit_bytes=VMEM_BYTES),
        name="store_results",
    )(*results)


def solution(mesh):
    placed = (
        P("seq", "section"),
        P("seq", "section"),
        P("seq", "section"),
        P("seq", "section"),
        P("section"),
        P("section"),
        P("seq"),
    )
    return jax.shard_map(
        functools.partial(on_device, mesh.shape["section"], mesh.shape["seq"]),
        mesh=mesh,
        in_specs=placed,
        out_specs=(P("seq", "section"),) * 4,
        check_vma=False,
    )
```
